256 devices in a mesh: occ: 32 (over y, x, core), pts: 8 (over z).
Axes of the slice: x: 4, y: 4, z: 8, core: 2. Of those that a mesh axis runs over, the one named last changes fastest.
Arguments:
- integrals: bfloat16 [32, 1024, 4608], P(None, 'occ'), may hold values from -0.0029296875 to 0.0029296875
- occupied_points: bfloat16 [1024, 6144], P('occ', 'pts'), may hold values from -6 to 6
- virtual_points: bfloat16 [4608, 6144], P('occ', 'pts'), may hold values from -6 to 6
Outputs:
- gram: float32 [6144, 6144], P('pts', 'occ')
The draws below stay inside these ranges and needn't reach their ends.
All inputs are finite; a program needn't handle non-finite values.
Results may differ from the reference program's by a relative error of at most 0.0003.
Values may be sent and summed in bfloat16 or wider, within the bound.
A program may use at most 128 MiB of HBM per device.

```python
import jax
import jax.numpy as jnp
from jax import lax

P_SIZE = 32
NV = 4608
NO = 1024
NQ = 6144


def levels(own_key, dims, shards, smallest, largest):
    factor_of = 1.0
    for position, blocks in shards:
        heights = jax.random.uniform(jax.random.fold_in(jax.random.fold_in(own_key, 6), position), (blocks,), jnp.float32, smallest / len(shards), largest / len(shards))
        factor_of = factor_of * jnp.repeat(jnp.exp(heights), dims[position] // blocks).reshape((-1,) + (1,) * (len(dims) - 1 - position))
    return factor_of


def centred(key, shape, scale, bound, cuts=(), dtype=jnp.bfloat16):
    array = scale * jax.random.normal(key, shape, jnp.float32)
    if cuts:
        array = array * levels(key, shape, cuts, -0.22, 0.18)
    return jnp.clip(array, -bound, bound).astype(dtype)


def setup_inputs(seed: int = 0) -> dict:
    keys = jax.random.split(jax.random.key(seed), 4)
    integrals = centred(keys[0], (P_SIZE, NO, NV), (NO * NV) ** -0.5, 0.0029296875, ((1, 32),))
    occupied_points = centred(keys[1], (NO, NQ), 1.0, 6.0, ((0, 32), (1, 8)))
    virtual_points = centred(keys[2], (NV, NQ), 1.0, 6.0, ((0, 32), (1, 8)))
    return {"integrals": integrals, "occupied_points": occupied_points, "virtual_points": virtual_points}


def reference(integrals, occupied_points, virtual_points):
    occupied_float = occupied_points.astype(jnp.float32)

    def one_row(integral_row):
        product = jnp.dot(integral_row, virtual_points, preferred_element_type=jnp.float32)
        return jnp.sum(product * occupied_float, axis=0)

    projection = lax.map(one_row, integrals)
    return jnp.dot(projection.T, projection, precision=lax.Precision.HIGHEST, preferred_element_type=jnp.float32)
```

```python
import functools

import jax
import jax.numpy as jnp
from jax import lax
from jax.experimental import pallas as pl
from jax.experimental.pallas import tpu as pltpu
from jax.sharding import PartitionSpec as P

MESH = pl.DeviceIdType.MESH
NX, NY, NZ = 4, 4, 8
PLANE = NX * NY * 2
CHUNK = 256
LANES = 128
TILE_P = 8


def split3(x):
    hi = x.astype(jnp.bfloat16)
    rest = x - hi.astype(jnp.float32)
    mid = rest.astype(jnp.bfloat16)
    low = (rest - mid.astype(jnp.float32)).astype(jnp.bfloat16)
    return hi, mid, low


def kernel(b_hbm, occ_hbm, v_hbm, out_ref, b_ref, occ_ref, panel, part, gathered, total, rows_y, cols_y,
           local_sem, recv_sem, send_sem, rs_send, rs_recv, ag_send, ag_recv, col_recv):
    nrows, width = v_hbm.shape
    nchunks = width // CHUNK
    tiles_q = width // LANES
    naux = part.shape[1]
    groups = naux // TILE_P
    owners = tiles_q * groups
    occ_local = occ_ref.shape[0]

    me = lax.axis_index("occ")
    z = lax.axis_index("pts")
    core = lax.rem(me, 2)
    x = lax.rem(me // 2, NX)
    y = me // (2 * NX)
    first = x + core * (y - x)
    second = y + core * (x - y)

    def occ_of(f, s):
        f = lax.rem(first + f + 4, 4)
        s = lax.rem(second + s + 4, 4)
        return (s * (4 - 3 * core) + f * (1 + 3 * core)) * 2 + core

    def at(f, s):
        return {"occ": occ_of(f, s), "pts": z}

    sibling = {"occ": me + 1 - 2 * core, "pts": z}

    home = me // 4
    tile = lax.rem(me, 4)
    first_block = 3 * (tile // 2) + lax.rem(tile, 2)
    is_home = home == z
    is_owner = me < owners
    my_block = me // groups
    my_group = lax.rem(me, groups)
    both = lax.rem(my_block, 3) == 1

    barrier = pltpu.get_barrier_semaphore()

    def greet(n, _):
        pl.semaphore_signal(barrier, inc=1, device_id={"occ": lax.rem(me + n, PLANE), "pts": z}, device_id_type=MESH)
        return 0

    lax.fori_loop(1, PLANE, greet, 0)

    @pl.when(jnp.logical_not(is_home))
    def _():
        def greet_owner(n, _):
            pl.semaphore_signal(
                barrier, inc=1, device_id={"occ": first_block * groups + n, "pts": home}, device_id_type=MESH
            )
            return 0

        lax.fori_loop(0, 2 * groups, greet_owner, 0)

    b_copy = pltpu.make_async_copy(b_hbm, b_ref, local_sem.at[0])
    occ_copy = pltpu.make_async_copy(occ_hbm, occ_ref, local_sem.at[1])
    own_copies = [
        pltpu.make_async_copy(
            v_hbm.at[:, pl.ds(k * CHUNK, CHUNK)], panel.at[k, pl.ds(me * nrows, nrows)], local_sem.at[2 + k]
        )
        for k in range(nchunks)
    ]
    for copy in own_copies:
        copy.start()
    b_copy.start()
    occ_copy.start()

    peers = PLANE - 1 + jnp.where(is_owner, (NZ - 1) * jnp.where(both, 2, 1), 0)
    pl.semaphore_wait(barrier, peers)

    half = nrows // 32 * 16 + 16 if nrows % 32 else nrows // 2

    def push(k, row, count, device, slot, src=None):
        block = panel.at[k, pl.ds(row, count)]
        pltpu.make_async_remote_copy(
            src_ref=block if src is None else src,
            dst_ref=block,
            send_sem=send_sem.at[k],
            recv_sem=recv_sem.at[k, slot],
            device_id=device,
            device_id_type=MESH,
        ).start()

    def row_of(f, s):
        return pl.multiple_of(occ_of(f, s) * nrows, 16)

    def shard(k, f, s, device, slot):
        push(k, row_of(f, s), nrows, device, slot)

    def arrived(k, slot, count):
        block = panel.at[k, pl.ds(0, count)]
        pltpu.make_async_copy(block, block, recv_sem.at[k, slot]).wait()

    def phase0(k):
        src = v_hbm.at[:, pl.ds(k * CHUNK, CHUNK)]
        row = row_of(0, 0)
        push(k, row, nrows, at(1, 0), 0, src)
        push(k, row, nrows, at(-1, 0), 1, src)
        push(k, row, nrows, sibling, 10, src)

    def phase1(k):
        own_copies[k].wait()
        arrived(k, 0, nrows)
        push(k, row_of(-1, 0), half, at(1, 0), 2)
        arrived(k, 1, nrows)
        push(k, pl.multiple_of(row_of(1, 0) + half, 16), nrows - half, at(-1, 0), 3)
        for f in (0, -1):
            shard(k, f, 0, at(0, 1), 4)
        shard(k, 1, 0, at(0, -1), 6)
        shard(k, 1, 0, at(0, 1), 5)
        for f in (0, -1):
            shard(k, f, 0, at(0, -1), 7)
        shard(k, 1, 0, sibling, 10)
        shard(k, -1, 0, sibling, 10)

    def phase2(k):
        arrived(k, 2, half)
        arrived(k, 3, nrows - half)
        shard(k, 2, 0, at(0, -1), 6)
        shard(k, 2, 0, at(0, 1), 5)
        shard(k, 2, 0, sibling, 10)

    def phase3a(k):
        arrived(k, 4, 2 * nrows)
        for f in (0, -1):
            shard(k, f, -1, at(0, 1), 8)
        arrived(k, 6, 2 * nrows)
        for f in (1, 2):
            shard(k, f, 1, at(0, -1), 9)
        for f in (0, -1):
            shard(k, f, -1, sibling, 10)
        for f in (1, 2):
            shard(k, f, 1, sibling, 10)

    def phase3b(k):
        arrived(k, 5, 2 * nrows)
        for f in (1, 2):
            shard(k, f, -1, sibling, 10)
        arrived(k, 7, 2 * nrows)
        for f in (0, -1):
            shard(k, f, 1, sibling, 10)

    def phase4(k):
        arrived(k, 8, 2 * nrows)
        for f in (0, -1):
            shard(k, f, 2, sibling, 10)
        arrived(k, 9, 2 * nrows)
        for f in (1, 2):
            shard(k, f, 2, sibling, 10)

    def phase5(k):
        arrived(k, 10, PLANE // 2 * nrows)

    def send_tile(qb, g):
        owner = qb * groups + g

        @pl.when(me != owner)
        def _():
            pltpu.make_async_remote_copy(
                src_ref=part.at[qb, pl.ds(g * TILE_P, TILE_P)],
                dst_ref=gathered.at[lax.rem(me - owner + PLANE, PLANE) - 1],
                send_sem=rs_send,
                recv_sem=rs_recv,
                device_id={"occ": owner, "pts": z},
                device_id_type=MESH,
            ).start()

    def compute(k, g):
        depth = TILE_P * occ_local
        t = jnp.dot(b_ref[pl.ds(g * depth, depth), :], panel[k], preferred_element_type=jnp.float32)
        o = occ_ref[:, pl.ds(k * CHUNK, CHUNK)].astype(jnp.float32)
        sums = jnp.sum(t.reshape(TILE_P, occ_local, CHUNK) * o[None], axis=1)
        for h in range(CHUNK // LANES):
            part[k * (CHUNK // LANES) + h, pl.ds(g * TILE_P, TILE_P)] = sums[:, h * LANES:(h + 1) * LANES]
        for h in range(CHUNK // LANES):
            send_tile(k * (CHUNK // LANES) + h, g)

    for k in range(nchunks):
        phase0(k)
    phase1(0)
    phase2(0)
    phase1(1)
    phase2(1)
    phase3a(0)
    phase3b(0)
    phase1(2)
    phase2(2)
    phase4(0)
    b_copy.wait()
    occ_copy.wait()
    phase5(0)
    compute(0, 0)
    phase3a(1)
    compute(0, 1)
    phase3b(1)
    compute(0, 2)
    compute(0, 3)
    phase4(1)
    phase3a(2)
    phase5(1)
    compute(1, 0)
    phase3b(2)
    compute(1, 1)
    compute(1, 2)
    compute(1, 3)
    phase4(2)
    phase5(2)
    for g in range(groups):
        compute(2, g)

    def rs_bytes(count):
        block = gathered.at[pl.ds(0, count)]
        pltpu.make_async_copy(block, block, rs_recv).wait()

    @pl.when(is_owner)
    def _():
        rs_bytes(PLANE - 1)
        acc = part[my_block, pl.ds(pl.multiple_of(my_group * TILE_P, TILE_P), TILE_P)]
        for n in range(PLANE - 1):
            acc = acc + gathered[n]
        total[...] = acc
        rows_y[my_block, pl.ds(pl.multiple_of(my_group * TILE_P, TILE_P), TILE_P)] = acc

        def to_column(tile_index):
            slot = my_block - (3 * (tile_index // 2) + lax.rem(tile_index, 2))

            def send(n, _):
                pltpu.make_async_remote_copy(
                    src_ref=total,
                    dst_ref=cols_y.at[slot, pl.ds(pl.multiple_of(my_group * TILE_P, TILE_P), TILE_P)],
                    send_sem=ag_send,
                    recv_sem=col_recv,
                    device_id={"occ": z * 4 + tile_index, "pts": lax.rem(z + n, NZ)},
                    device_id_type=MESH,
                ).start()
                return 0

            lax.fori_loop(1, NZ, send, 0)

        low_tile = 2 * (my_block // 3) + lax.rem(my_block, 3) // 2
        to_column(low_tile)

        @pl.when(both)
        def _():
            to_column(low_tile + 1)

        def to_plane(n, _):
            pltpu.make_async_remote_copy(
                src_ref=total,
                dst_ref=rows_y.at[my_block, pl.ds(pl.multiple_of(my_group * TILE_P, TILE_P), TILE_P)],
                send_sem=ag_send,
                recv_sem=ag_recv,
                device_id={"occ": lax.rem(me + n, PLANE), "pts": z},
                device_id_type=MESH,
            ).start()
            return 0

        lax.fori_loop(1, PLANE, to_plane, 0)

    def wait_tiles(sem, count):
        block = gathered.at[pl.ds(0, count)]
        pltpu.make_async_copy(block, block, sem).wait()

    @pl.when(is_owner)
    def _():
        wait_tiles(ag_recv, owners - 1)

    @pl.when(jnp.logical_not(is_owner))
    def _():
        wait_tiles(ag_recv, owners)

    @pl.when(is_home)
    def _():
        cols_y[...] = rows_y[pl.ds(first_block, 2)]

    @pl.when(jnp.logical_not(is_home))
    def _():
        wait_tiles(col_recv, 2 * groups)

    odd = lax.rem(me, 2) == 1
    cols = jnp.concatenate([cols_y[0], cols_y[1]], axis=1)
    cols = jnp.where(odd, pltpu.roll(cols, cols.shape[1] - LANES // 2, 1), cols)
    c1, c2, c3 = split3(cols)
    right = jnp.concatenate([c1, c2, c1, c2, c3, c1], axis=0)
    for qb in range(tiles_q):
        r1, r2, r3 = split3(rows_y[qb])
        left = jnp.concatenate([r1, r1, r2, r2, r1, r3], axis=0)
        g = lax.dot_general(left, right, (((0,), (0,)), ((), ())), preferred_element_type=jnp.float32)
        out_ref[pl.ds(qb * LANES, LANES), :] = g[:, :out_ref.shape[1]]

    for k in range(nchunks):
        sent = panel.at[k, pl.ds(0, (PLANE - 1) * nrows)]
        pltpu.make_async_copy(sent, sent, send_sem.at[k]).wait()

    @pl.when(is_owner)
    def _():
        wait_tiles(rs_send, owners - 1)
        wait_tiles(ag_send, PLANE - 1)
        wait_tiles(ag_send, NZ - 1)

        @pl.when(both)
        def _():
            wait_tiles(ag_send, NZ - 1)

    @pl.when(jnp.logical_not(is_owner))
    def _():
        wait_tiles(rs_send, owners)


def body(integrals, occupied_points, virtual_points):
    naux, occ_local, nvirt = integrals.shape
    nrows, width = virtual_points.shape
    nchunks = width // CHUNK
    tiles_q = width // LANES
    tile_width = width * NZ // PLANE
    flat = integrals.reshape(naux * occ_local, nvirt)
    anywhere = pl.BlockSpec(memory_space=pl.ANY)
    return pl.pallas_call(
        kernel,
        out_shape=jax.ShapeDtypeStruct((width, tile_width), jnp.float32),
        in_specs=[anywhere] * 3,
        out_specs=pl.BlockSpec(memory_space=pltpu.VMEM),
        scratch_shapes=[
            pltpu.VMEM((naux * occ_local, nvirt), jnp.bfloat16),
            pltpu.VMEM((occ_local, width), jnp.bfloat16),
            pltpu.VMEM((nchunks, nvirt, CHUNK), jnp.bfloat16),
            pltpu.VMEM((tiles_q, naux, LANES), jnp.float32),
            pltpu.VMEM((PLANE, TILE_P, LANES), jnp.float32),
            pltpu.VMEM((TILE_P, LANES), jnp.float32),
            pltpu.VMEM((tiles_q, naux, LANES), jnp.float32),
            pltpu.VMEM((2, naux, LANES), jnp.float32),
            pltpu.SemaphoreType.DMA((2 + nchunks,)),
            pltpu.SemaphoreType.DMA((nchunks, 11)),
            pltpu.SemaphoreType.DMA((nchunks,)),
            pltpu.SemaphoreType.DMA,
            pltpu.SemaphoreType.DMA,
            pltpu.SemaphoreType.DMA,
            pltpu.SemaphoreType.DMA,
            pltpu.SemaphoreType.DMA,
        ],
        compiler_params=pltpu.CompilerParams(
            collective_id=0, has_side_effects=True, vmem_limit_bytes=56 * 2**20
        ),
        cost_estimate=pl.CostEstimate(
            flops=2 * naux * occ_local * nvirt * width, bytes_accessed=12 * 2**20, transcendentals=0
        ),
    )(flat, occupied_points, virtual_points)


def solution(mesh):
    return jax.shard_map(
        body,
        mesh=mesh,
        in_specs=(P(None, "occ", None), P("occ", "pts"), P("occ", "pts")),
        out_specs=P("pts", "occ"),
        check_vma=False,
    )
```

```python
import functools

import jax
import jax.numpy as jnp
from jax import lax
from jax.experimental import pallas as pl
from jax.experimental.pallas import tpu as pltpu
from jax.sharding import PartitionSpec as P

MESH = pl.DeviceIdType.MESH
NX, NY, NZ = 4, 4, 8
PLANE = NX * NY * 2
CHUNK = 256
LANES = 128
TILE_P = 8


def split3(x):
    hi = x.astype(jnp.bfloat16)
    rest = x - hi.astype(jnp.float32)
    mid = rest.astype(jnp.bfloat16)
    low = (rest - mid.astype(jnp.float32)).astype(jnp.bfloat16)
    return hi, mid, low


def kernel(b_hbm, occ_hbm, v_hbm, rows_y, cols_y, b_ref, occ_ref, panel, part, gathered, total,
           local_sem, recv_sem, send_sem, rs_send, rs_recv, ag_send, ag_recv, col_recv, z_token):
    nrows, width = v_hbm.shape
    nchunks = width // CHUNK
    blocks = CHUNK // LANES
    naux = part.shape[1]
    groups = naux // TILE_P
    tiles = blocks * groups
    last = nchunks - 1
    occ_local = occ_ref.shape[0]

    me = lax.axis_index("occ")
    z = lax.axis_index("pts")
    core = lax.rem(me, 2)
    x = lax.rem(me // 2, NX)
    y = me // (2 * NX)
    first = x + core * (y - x)
    second = y + core * (x - y)

    def occ_of(f, s):
        f = lax.rem(first + f + 4, 4)
        s = lax.rem(second + s + 4, 4)
        return (s * (4 - 3 * core) + f * (1 + 3 * core)) * 2 + core

    def at(f, s):
        return {"occ": occ_of(f, s), "pts": z}

    sibling = {"occ": me + 1 - 2 * core, "pts": z}
    above = {"occ": me, "pts": lax.rem(z + 1, NZ)}
    below = {"occ": me, "pts": lax.rem(z + NZ - 1, NZ)}

    home = me // 4
    tile = lax.rem(me, 4)
    first_block = 3 * (tile // 2) + lax.rem(tile, 2)
    is_home = home == z

    my_chunk = lax.rem(me, 4)
    my_tile = me // 4
    home_x = 2 * lax.rem(z, 2) + 1
    home_y = z // 2
    last_tile = 2 * lax.rem(x + NX - home_x, NX) + core

    barrier = pltpu.get_barrier_semaphore()
    neighbours = [at(1, 0), at(-1, 0), at(0, 1), at(0, -1), sibling, above, below]
    for device in neighbours:
        pl.semaphore_signal(barrier, inc=1, device_id=device, device_id_type=MESH)

    b_copy = pltpu.make_async_copy(b_hbm, b_ref, local_sem.at[0])
    occ_copy = pltpu.make_async_copy(occ_hbm, occ_ref, local_sem.at[1])
    own_copies = [
        pltpu.make_async_copy(
            v_hbm.at[:, pl.ds(k * CHUNK, CHUNK)], panel.at[k, pl.ds(me * nrows, nrows)], local_sem.at[2 + k]
        )
        for k in range(nchunks)
    ]
    for copy in own_copies:
        copy.start()
    b_copy.start()
    occ_copy.start()

    pl.semaphore_wait(barrier, len(neighbours))

    def z_signal(r):
        for device in (above, below):
            pl.semaphore_signal(z_token.at[r], inc=1, device_id=device, device_id_type=MESH)

    def z_wait(r):
        pl.semaphore_wait(z_token.at[r], 2)

    half = nrows // 32 * 16 + 16 if nrows % 32 else nrows // 2

    def push(k, row, count, device, slot, src=None):
        block = panel.at[k, pl.ds(row, count)]
        pltpu.make_async_remote_copy(
            src_ref=block if src is None else src,
            dst_ref=block,
            send_sem=send_sem.at[k],
            recv_sem=recv_sem.at[k, slot],
            device_id=device,
            device_id_type=MESH,
        ).start()

    def row_of(f, s):
        return pl.multiple_of(occ_of(f, s) * nrows, 16)

    def shard(k, f, s, device, slot):
        push(k, row_of(f, s), nrows, device, slot)

    def arrived(k, slot, count):
        block = panel.at[k, pl.ds(0, count)]
        pltpu.make_async_copy(block, block, recv_sem.at[k, slot]).wait()

    def phase0(k):
        src = v_hbm.at[:, pl.ds(k * CHUNK, CHUNK)]
        row = row_of(0, 0)
        push(k, row, nrows, at(1, 0), 0, src)
        push(k, row, nrows, at(-1, 0), 1, src)
        push(k, row, nrows, sibling, 10, src)

    def halves(k):
        arrived(k, 0, nrows)
        push(k, row_of(-1, 0), half, at(1, 0), 2)
        arrived(k, 1, nrows)
        push(k, pl.multiple_of(row_of(1, 0) + half, 16), nrows - half, at(-1, 0), 3)

    def bulk(k):
        own_copies[k].wait()
        shard(k, 1, 0, at(0, -1), 6)
        for f in (0, -1):
            shard(k, f, 0, at(0, 1), 4)
        for f in (0, -1):
            shard(k, f, 0, at(0, -1), 7)
        shard(k, 1, 0, at(0, 1), 5)
        shard(k, 1, 0, sibling, 10)
        shard(k, -1, 0, sibling, 10)

    def opposite(k):
        arrived(k, 2, half)
        arrived(k, 3, nrows - half)
        shard(k, 2, 0, at(0, -1), 11)
        shard(k, 2, 0, at(0, 1), 5)
        shard(k, 2, 0, sibling, 10)

    def phase3(k):
        arrived(k, 4, 2 * nrows)
        for f in (0, -1):
            shard(k, f, -1, at(0, 1), 8)
        arrived(k, 6, nrows)
        shard(k, 1, 1, at(0, -1), 9)
        for f in (0, -1):
            shard(k, f, -1, sibling, 10)
        shard(k, 1, 1, sibling, 10)
        arrived(k, 11, nrows)
        shard(k, 2, 1, at(0, -1), 9)
        shard(k, 2, 1, sibling, 10)
        arrived(k, 5, 2 * nrows)
        for f in (1, 2):
            shard(k, f, -1, sibling, 10)
        arrived(k, 7, 2 * nrows)
        for f in (0, -1):
            shard(k, f, 1, sibling, 10)

    def phase4(k):
        arrived(k, 8, 2 * nrows)
        for f in (0, -1):
            shard(k, f, 2, sibling, 10)
        arrived(k, 9, 2 * nrows)
        for f in (1, 2):
            shard(k, f, 2, sibling, 10)

    def phase5(k):
        arrived(k, 10, PLANE // 2 * nrows)

    def compute(k, g):
        depth = TILE_P * occ_local
        t = jnp.dot(b_ref[pl.ds(g * depth, depth), :], panel[k], preferred_element_type=jnp.float32)
        o = occ_ref[:, pl.ds(k * CHUNK, CHUNK)].astype(jnp.float32)
        sums = jnp.sum(t.reshape(TILE_P, occ_local, CHUNK) * o[None], axis=1)
        for h in range(blocks):
            part[k * blocks + h, pl.ds(g * TILE_P, TILE_P)] = sums[:, h * LANES:(h + 1) * LANES]

    def multiply(k):
        for g in range(groups):
            compute(k, g)

    def tile_of(ref, k, t):
        return ref.at[k * blocks + t // groups, pl.ds(pl.multiple_of(lax.rem(t, groups) * TILE_P, TILE_P), TILE_P)]

    def send(src, dst, ssem, rsem, occ, pts):
        pltpu.make_async_remote_copy(
            src_ref=src, dst_ref=dst, send_sem=ssem, recv_sem=rsem,
            device_id={"occ": occ, "pts": pts}, device_id_type=MESH,
        ).start()

    def send_part(k, t, owner):
        send(tile_of(part, k, t), gathered.at[k, lax.rem(me - owner + PLANE, PLANE) - 1],
             rs_send, rs_recv.at[k], owner, z)

    def scatter(k):
        def step(n, _):
            t = lax.rem(my_tile + n, tiles)
            send_part(k, t, t * 4 + k)
            return 0

        lax.fori_loop(jnp.where(my_chunk == k, 1, 0), tiles, step, 0)

    def scatter_last():
        def step(n, _):
            t = n // NY
            row = lax.rem(y + lax.rem(n, NY), NY)
            owner = (row * NX + lax.rem(home_x + t // 2, NX)) * 2 + lax.rem(t, 2)

            @pl.when(owner != me)
            def _():
                send_part(last, t, owner)

            return 0

        lax.fori_loop(0, tiles * NY, step, 0)

    def wait_tiles(sem, count):
        block = gathered.at[0, pl.ds(0, count)]
        pltpu.make_async_copy(block, block, sem).wait()

    def add_up(k, t):
        wait_tiles(rs_recv.at[k], PLANE - 1)
        acc = tile_of(part, k, t)[...]
        for n in range(PLANE - 1):
            acc = acc + gathered[k, n]
        total[k] = acc
        tile_of(rows_y, k, t)[...] = acc

    def to_columns(k, t):
        block = k * blocks + t // groups
        low = 2 * (block // 3) + lax.rem(block, 3) // 2
        count = jnp.where(lax.rem(block, 3) == 1, 2, 1)

        def step(n, _):
            user = low + n // (NZ - 1)
            slot = block - (3 * (user // 2) + lax.rem(user, 2))
            send(total.at[k],
                 cols_y.at[slot, pl.ds(pl.multiple_of(lax.rem(t, groups) * TILE_P, TILE_P), TILE_P)],
                 ag_send, col_recv, z * 4 + user, lax.rem(z + 1 + lax.rem(n, NZ - 1), NZ))
            return 0

        lax.fori_loop(0, count * (NZ - 1), step, 0)

    def spread(k):
        add_up(k, my_tile)
        to_columns(k, my_tile)

        def step(n, _):
            send(total.at[k], tile_of(rows_y, k, my_tile), ag_send, ag_recv.at[k], lax.rem(me + n, PLANE), z)
            return 0

        lax.fori_loop(1, PLANE, step, 0)

    def spread_last():
        add_up(last, last_tile)

        @pl.when(y == home_y)
        def _():
            to_columns(last, last_tile)

        def step(n, _):
            send(total.at[last], tile_of(rows_y, last, last_tile), ag_send, ag_recv.at[last],
                 y * 2 * NX + lax.rem(x * 2 + core + n, 2 * NX), z)
            return 0

        lax.fori_loop(1, 2 * NX, step, 0)

    def columns_sent(k, t):
        wait_tiles(ag_send, NZ - 1)

        @pl.when(lax.rem(k * blocks + t // groups, 3) == 1)
        def _():
            wait_tiles(ag_send, NZ - 1)

    z_signal(0)
    for k in range(nchunks):
        phase0(k)
    halves(0)
    bulk(0)
    halves(1)
    halves(2)
    z_wait(0)
    z_signal(1)
    opposite(0)
    bulk(1)
    opposite(1)
    opposite(2)
    phase3(0)
    z_wait(1)
    z_signal(2)
    bulk(2)
    phase3(1)
    b_copy.wait()
    occ_copy.wait()
    phase4(0)
    phase5(0)
    multiply(0)
    z_wait(2)
    scatter(0)
    phase3(2)
    phase4(1)
    phase5(1)
    multiply(1)
    scatter(1)
    phase4(2)
    phase5(2)
    multiply(2)
    scatter_last()

    for k in range(last):
        @pl.when(my_chunk == k)
        def _():
            spread(k)

    spread_last()

    for k in range(last):
        @pl.when(my_chunk == k)
        def _():
            wait_tiles(ag_recv.at[k], tiles - 1)

        @pl.when(my_chunk != k)
        def _():
            wait_tiles(ag_recv.at[k], tiles)

    wait_tiles(ag_recv.at[last], tiles - 1)

    @pl.when(is_home)
    def _():
        cols_y[...] = rows_y[pl.ds(first_block, 2)]

    @pl.when(jnp.logical_not(is_home))
    def _():
        wait_tiles(col_recv, 2 * groups)

    for k in range(nchunks):
        sent = panel.at[k, pl.ds(0, (PLANE - 1) * nrows)]
        pltpu.make_async_copy(sent, sent, send_sem.at[k]).wait()

    wait_tiles(rs_send, PLANE - 1)
    for k in range(last):
        @pl.when(my_chunk == k)
        def _():
            wait_tiles(rs_send, tiles - 1)
            wait_tiles(ag_send, PLANE - 1)
            columns_sent(k, my_tile)

        @pl.when(my_chunk != k)
        def _():
            wait_tiles(rs_send, tiles)

    wait_tiles(ag_send, tiles - 1)

    @pl.when(y == home_y)
    def _():
        columns_sent(last, last_tile)


def gram_kernel(rows_ref, cols_ref, out_ref):
    odd = lax.rem(lax.axis_index("occ"), 2) == 1
    cols = jnp.concatenate([cols_ref[0], cols_ref[1]], axis=1)
    cols = jnp.where(odd, pltpu.roll(cols, cols.shape[1] - LANES // 2, 1), cols)
    c1, c2, c3 = split3(cols)
    right = jnp.concatenate([c1, c2, c1, c2, c3, c1], axis=0)
    for qb in range(rows_ref.shape[0]):
        r1, r2, r3 = split3(rows_ref[qb])
        left = jnp.concatenate([r1, r1, r2, r2, r1, r3], axis=0)
        g = lax.dot_general(left, right, (((0,), (0,)), ((), ())), preferred_element_type=jnp.float32)
        out_ref[pl.ds(qb * LANES, LANES), :] = g[:, :out_ref.shape[1]]


def body(integrals, occupied_points, virtual_points):
    naux, occ_local, nvirt = integrals.shape
    nrows, width = virtual_points.shape
    nchunks = width // CHUNK
    tiles_q = width // LANES
    tile_width = width * NZ // PLANE
    flat = integrals.reshape(naux * occ_local, nvirt)
    anywhere = pl.BlockSpec(memory_space=pl.ANY)
    vmem = pl.BlockSpec(memory_space=pltpu.VMEM)
    rows, cols = pl.pallas_call(
        kernel,
        out_shape=[
            jax.ShapeDtypeStruct((tiles_q, naux, LANES), jnp.float32),
            jax.ShapeDtypeStruct((2, naux, LANES), jnp.float32),
        ],
        in_specs=[anywhere] * 3,
        out_specs=[vmem] * 2,
        scratch_shapes=[
            pltpu.VMEM((naux * occ_local, nvirt), jnp.bfloat16),
            pltpu.VMEM((occ_local, width), jnp.bfloat16),
            pltpu.VMEM((nchunks, nvirt, CHUNK), jnp.bfloat16),
            pltpu.VMEM((tiles_q, naux, LANES), jnp.float32),
            pltpu.VMEM((nchunks, PLANE, TILE_P, LANES), jnp.float32),
            pltpu.VMEM((nchunks, TILE_P, LANES), jnp.float32),
            pltpu.SemaphoreType.DMA((2 + nchunks,)),
            pltpu.SemaphoreType.DMA((nchunks, 12)),
            pltpu.SemaphoreType.DMA((nchunks,)),
            pltpu.SemaphoreType.DMA,
            pltpu.SemaphoreType.DMA((nchunks,)),
            pltpu.SemaphoreType.DMA,
            pltpu.SemaphoreType.DMA((nchunks,)),
            pltpu.SemaphoreType.DMA,
            pltpu.SemaphoreType.REGULAR((3,)),
        ],
        compiler_params=pltpu.CompilerParams(
            collective_id=0, has_side_effects=True, vmem_limit_bytes=56 * 2**20
        ),
        cost_estimate=pl.CostEstimate(
            flops=2 * naux * occ_local * nvirt * width, bytes_accessed=12 * 2**20, transcendentals=0
        ),
        name="project",
    )(flat, occupied_points, virtual_points)
    return pl.pallas_call(
        gram_kernel,
        out_shape=jax.ShapeDtypeStruct((width, tile_width), jnp.float32),
        in_specs=[vmem] * 2,
        out_specs=vmem,
        cost_estimate=pl.CostEstimate(
            flops=12 * naux * width * tile_width, bytes_accessed=2**20, transcendentals=0
        ),
        name="gram",
    )(rows, cols)


def solution(mesh):
    return jax.shard_map(
        body,
        mesh=mesh,
        in_specs=(P(None, "occ", None), P("occ", "pts"), P("occ", "pts")),
        out_specs=P("pts", "occ"),
        check_vma=False,
    )
```

```python
import functools

import jax
import jax.numpy as jnp
from jax import lax
from jax.experimental import pallas as pl
from jax.experimental.pallas import tpu as pltpu
from jax.sharding import PartitionSpec as P

MESH = pl.DeviceIdType.MESH
NX, NY, NZ = 4, 4, 8
PLANE = NX * NY * 2
CHUNK = 256
LANES = 128
TILE_P = 8


def split3(x):
    hi = x.astype(jnp.bfloat16)
    rest = x - hi.astype(jnp.float32)
    mid = rest.astype(jnp.bfloat16)
    low = (rest - mid.astype(jnp.float32)).astype(jnp.bfloat16)
    return hi, mid, low


def kernel(b_hbm, occ_hbm, v_hbm, rows_y, cols_y, b_ref, occ_ref, panel, part, gathered, total,
           local_sem, recv_sem, send_sem, rs_send, rs_recv, ag_send, ag_recv, col_recv, z_token):
    nrows, width = v_hbm.shape
    nchunks = width // CHUNK
    blocks = CHUNK // LANES
    naux = part.shape[1]
    groups = naux // TILE_P
    tiles = blocks * groups
    last = nchunks - 1
    occ_local = occ_ref.shape[0]

    me = lax.axis_index("occ")
    z = lax.axis_index("pts")
    core = lax.rem(me, 2)
    x = lax.rem(me // 2, NX)
    y = me // (2 * NX)
    first = x + core * (y - x)
    second = y + core * (x - y)

    def occ_of(f, s):
        f = lax.rem(first + f + 4, 4)
        s = lax.rem(second + s + 4, 4)
        return (s * (4 - 3 * core) + f * (1 + 3 * core)) * 2 + core

    def at(f, s):
        return {"occ": occ_of(f, s), "pts": z}

    sibling = {"occ": me + 1 - 2 * core, "pts": z}
    above = {"occ": me, "pts": lax.rem(z + 1, NZ)}
    below = {"occ": me, "pts": lax.rem(z + NZ - 1, NZ)}

    home = me // 4
    tile = lax.rem(me, 4)
    first_block = 3 * (tile // 2) + lax.rem(tile, 2)
    is_home = home == z

    my_chunk = lax.rem(me, 4)
    my_tile = me // 4
    home_x = 2 * lax.rem(z, 2) + 1
    home_y = z // 2
    home_dy = lax.rem(y + NY - home_y, NY)
    last_tile = 2 * lax.rem(x + NX - home_x + 2 * home_dy, NX) + core
    sends_columns = jnp.logical_or(
        jnp.logical_and(home_dy == 0, last_tile // 2 != 2), jnp.logical_and(home_dy == 1, last_tile // 2 == 2)
    )

    barrier = pltpu.get_barrier_semaphore()
    neighbours = [at(1, 0), at(-1, 0), at(0, 1), at(0, -1), sibling, above, below]
    for device in neighbours:
        pl.semaphore_signal(barrier, inc=1, device_id=device, device_id_type=MESH)

    b_copy = pltpu.make_async_copy(b_hbm, b_ref, local_sem.at[0])
    occ_copy = pltpu.make_async_copy(occ_hbm, occ_ref, local_sem.at[1])
    own_copies = [
        pltpu.make_async_copy(
            v_hbm.at[:, pl.ds(k * CHUNK, CHUNK)], panel.at[k, pl.ds(me * nrows, nrows)], local_sem.at[2 + k]
        )
        for k in range(nchunks)
    ]
    for copy in own_copies:
        copy.start()
    b_copy.start()
    occ_copy.start()

    pl.semaphore_wait(barrier, len(neighbours))

    def z_signal(r):
        for device in (above, below):
            pl.semaphore_signal(z_token.at[r], inc=1, device_id=device, device_id_type=MESH)

    def z_wait(r):
        pl.semaphore_wait(z_token.at[r], 2)

    half = nrows // 32 * 16 + 16 if nrows % 32 else nrows // 2

    def push(k, row, count, device, slot, src=None):
        block = panel.at[k, pl.ds(row, count)]
        pltpu.make_async_remote_copy(
            src_ref=block if src is None else src,
            dst_ref=block,
            send_sem=send_sem.at[k],
            recv_sem=recv_sem.at[k, slot],
            device_id=device,
            device_id_type=MESH,
        ).start()

    def row_of(f, s):
        return pl.multiple_of(occ_of(f, s) * nrows, 16)

    def shard(k, f, s, device, slot):
        push(k, row_of(f, s), nrows, device, slot)

    def arrived(k, slot, count):
        block = panel.at[k, pl.ds(0, count)]
        pltpu.make_async_copy(block, block, recv_sem.at[k, slot]).wait()

    def phase0(k):
        src = v_hbm.at[:, pl.ds(k * CHUNK, CHUNK)]
        row = row_of(0, 0)
        push(k, row, nrows, at(1, 0), 0, src)
        push(k, row, nrows, at(-1, 0), 1, src)
        push(k, row, nrows, sibling, 10, src)

    def halves(k):
        arrived(k, 0, nrows)
        push(k, row_of(-1, 0), half, at(1, 0), 2)
        arrived(k, 1, nrows)
        push(k, pl.multiple_of(row_of(1, 0) + half, 16), nrows - half, at(-1, 0), 3)

    def bulk(k):
        own_copies[k].wait()
        shard(k, 1, 0, at(0, -1), 6)
        for f in (0, -1):
            shard(k, f, 0, at(0, 1), 4)
        for f in (0, -1):
            shard(k, f, 0, at(0, -1), 7)
        shard(k, 1, 0, at(0, 1), 5)
        shard(k, 1, 0, sibling, 10)
        shard(k, -1, 0, sibling, 10)

    def opposite(k):
        arrived(k, 2, half)
        arrived(k, 3, nrows - half)
        shard(k, 2, 0, at(0, -1), 11)
        shard(k, 2, 0, at(0, 1), 5)
        shard(k, 2, 0, sibling, 10)

    def phase3a(k):
        arrived(k, 4, 2 * nrows)
        for f in (0, -1):
            shard(k, f, -1, at(0, 1), 8)
        arrived(k, 6, nrows)
        shard(k, 1, 1, at(0, -1), 9)
        for f in (0, -1):
            shard(k, f, -1, sibling, 10)
        shard(k, 1, 1, sibling, 10)

    def phase3b(k):
        arrived(k, 11, nrows)
        shard(k, 2, 1, at(0, -1), 9)
        shard(k, 2, 1, sibling, 10)

    def phase3c(k):
        arrived(k, 5, 2 * nrows)
        for f in (1, 2):
            shard(k, f, -1, sibling, 10)
        arrived(k, 7, 2 * nrows)
        for f in (0, -1):
            shard(k, f, 1, sibling, 10)

    def phase3(k):
        phase3a(k)
        phase3b(k)
        phase3c(k)

    def phase4a(k):
        arrived(k, 8, 2 * nrows)
        for f in (0, -1):
            shard(k, f, 2, sibling, 10)

    def phase4b(k):
        arrived(k, 9, 2 * nrows)
        for f in (1, 2):
            shard(k, f, 2, sibling, 10)

    def phase4(k):
        phase4a(k)
        phase4b(k)

    def phase5(k):
        arrived(k, 10, PLANE // 2 * nrows)

    def compute(k, g):
        depth = TILE_P * occ_local
        t = jnp.dot(b_ref[pl.ds(g * depth, depth), :], panel[k], preferred_element_type=jnp.float32)
        o = occ_ref[:, pl.ds(k * CHUNK, CHUNK)].astype(jnp.float32)
        sums = jnp.sum(t.reshape(TILE_P, occ_local, CHUNK) * o[None], axis=1)
        for h in range(blocks):
            part[k * blocks + h, pl.ds(g * TILE_P, TILE_P)] = sums[:, h * LANES:(h + 1) * LANES]

    def multiply(k):
        for g in range(groups):
            compute(k, g)

    def tile_of(ref, k, t):
        if isinstance(t, int):
            return ref.at[k * blocks + t // groups, pl.ds(t % groups * TILE_P, TILE_P)]
        return ref.at[k * blocks + t // groups, pl.ds(pl.multiple_of(lax.rem(t, groups) * TILE_P, TILE_P), TILE_P)]

    def send(src, dst, ssem, rsem, occ, pts):
        pltpu.make_async_remote_copy(
            src_ref=src, dst_ref=dst, send_sem=ssem, recv_sem=rsem,
            device_id={"occ": occ, "pts": pts}, device_id_type=MESH,
        ).start()

    def send_part(k, t, owner):
        send(tile_of(part, k, t), gathered.at[k, lax.rem(me - owner + PLANE, PLANE) - 1],
             rs_send, rs_recv.at[k], owner, z)

    def scatter(k):
        def step(n, _):
            t = lax.rem(my_tile + n, tiles)
            send_part(k, t, t * 4 + k)
            return 0

        lax.fori_loop(jnp.where(my_chunk == k, 1, 0), tiles, step, 0)

    def scatter_last(first_group, last_group):
        for t in range(tiles):
            if not first_group <= t % groups < last_group:
                continue
            for r in range(NY):
                column = lax.rem(home_x + t // 2 + 2 * (home_dy + r), NX)
                owner = (lax.rem(y + r, NY) * NX + column) * 2 + t % 2
                if r:
                    send_part(last, t, owner)
                else:
                    @pl.when(last_tile != t)
                    def _():
                        send_part(last, t, owner)

    def wait_tiles(sem, count):
        block = gathered.at[0, pl.ds(0, count)]
        pltpu.make_async_copy(block, block, sem).wait()

    def add_up(k, t):
        wait_tiles(rs_recv.at[k], PLANE - 1)
        acc = tile_of(part, k, t)[...]
        for n in range(PLANE - 1):
            acc = acc + gathered[k, n]
        total[k] = acc
        tile_of(rows_y, k, t)[...] = acc

    def to_columns(k, t):
        block = k * blocks + t // groups
        low = 2 * (block // 3) + lax.rem(block, 3) // 2
        count = jnp.where(lax.rem(block, 3) == 1, 2, 1)

        def step(n, _):
            user = low + n // (NZ - 1)
            slot = block - (3 * (user // 2) + lax.rem(user, 2))
            send(total.at[k],
                 cols_y.at[slot, pl.ds(pl.multiple_of(lax.rem(t, groups) * TILE_P, TILE_P), TILE_P)],
                 ag_send, col_recv, z * 4 + user, lax.rem(z + 1 + lax.rem(n, NZ - 1), NZ))
            return 0

        lax.fori_loop(0, count * (NZ - 1), step, 0)

    def spread(k):
        add_up(k, my_tile)
        to_columns(k, my_tile)

        def step(n, _):
            send(total.at[k], tile_of(rows_y, k, my_tile), ag_send, ag_recv.at[k], lax.rem(me + n, PLANE), z)
            return 0

        lax.fori_loop(1, PLANE, step, 0)

    def spread_last():
        add_up(last, last_tile)

        @pl.when(sends_columns)
        def _():
            to_columns(last, last_tile)

        def step(n, _):
            send(total.at[last], tile_of(rows_y, last, last_tile), ag_send, ag_recv.at[last],
                 y * 2 * NX + lax.rem(x * 2 + core + n, 2 * NX), z)
            return 0

        lax.fori_loop(1, 2 * NX, step, 0)

    def columns_sent(k, t):
        wait_tiles(ag_send, NZ - 1)

        @pl.when(lax.rem(k * blocks + t // groups, 3) == 1)
        def _():
            wait_tiles(ag_send, NZ - 1)

    z_signal(0)
    phase0(0)
    phase0(1)
    phase0(2)
    halves(0)
    bulk(0)
    halves(1)
    halves(2)
    bulk(1)
    z_wait(0)
    z_signal(1)
    opposite(0)
    opposite(1)
    opposite(2)
    phase3(0)
    z_wait(1)
    z_signal(2)
    phase3(1)
    bulk(2)
    b_copy.wait()
    occ_copy.wait()
    phase4(0)
    phase5(0)
    compute(0, 0)
    compute(0, 1)
    compute(0, 2)
    compute(0, 3)
    phase3a(2)
    phase3b(2)
    phase3c(2)
    phase4(1)
    z_wait(2)
    scatter(0)
    phase5(1)
    compute(1, 0)
    compute(1, 1)
    phase4a(2)
    phase4b(2)
    compute(1, 2)
    compute(1, 3)
    phase5(2)
    scatter(1)
    multiply(2)
    scatter_last(0, groups)

    for k in range(last):
        @pl.when(my_chunk == k)
        def _():
            spread(k)

    spread_last()

    for k in range(last):
        @pl.when(my_chunk == k)
        def _():
            wait_tiles(ag_recv.at[k], tiles - 1)

        @pl.when(my_chunk != k)
        def _():
            wait_tiles(ag_recv.at[k], tiles)

    wait_tiles(ag_recv.at[last], tiles - 1)

    @pl.when(is_home)
    def _():
        cols_y[...] = rows_y[pl.ds(first_block, 2)]

    @pl.when(jnp.logical_not(is_home))
    def _():
        wait_tiles(col_recv, 2 * groups)

    for k in range(nchunks):
        sent = panel.at[k, pl.ds(0, (PLANE - 1) * nrows)]
        pltpu.make_async_copy(sent, sent, send_sem.at[k]).wait()

    wait_tiles(rs_send, PLANE - 1)
    for k in range(last):
        @pl.when(my_chunk == k)
        def _():
            wait_tiles(rs_send, tiles - 1)
            wait_tiles(ag_send, PLANE - 1)
            columns_sent(k, my_tile)

        @pl.when(my_chunk != k)
        def _():
            wait_tiles(rs_send, tiles)

    wait_tiles(ag_send, tiles - 1)

    @pl.when(sends_columns)
    def _():
        columns_sent(last, last_tile)


def gram_kernel(rows_ref, cols_ref, out_ref):
    odd = lax.rem(lax.axis_index("occ"), 2) == 1
    cols = jnp.concatenate([cols_ref[0], cols_ref[1]], axis=1)
    cols = jnp.where(odd, pltpu.roll(cols, cols.shape[1] - LANES // 2, 1), cols)
    c1, c2, c3 = split3(cols)
    right = jnp.concatenate([c1, c2, c1, c2, c3, c1], axis=0)
    for qb in range(rows_ref.shape[0]):
        r1, r2, r3 = split3(rows_ref[qb])
        left = jnp.concatenate([r1, r1, r2, r2, r1, r3], axis=0)
        g = lax.dot_general(right, left, (((0,), (0,)), ((), ())), preferred_element_type=jnp.float32)
        out_ref[:, pl.ds(qb * LANES, LANES)] = g[:out_ref.shape[0]]


def body(integrals, occupied_points, virtual_points):
    naux, occ_local, nvirt = integrals.shape
    nrows, width = virtual_points.shape
    nchunks = width // CHUNK
    tiles_q = width // LANES
    tile_width = width * NZ // PLANE
    flat = integrals.reshape(naux * occ_local, nvirt)
    anywhere = pl.BlockSpec(memory_space=pl.ANY)
    vmem = pl.BlockSpec(memory_space=pltpu.VMEM)
    rows, cols = pl.pallas_call(
        kernel,
        out_shape=[
            jax.ShapeDtypeStruct((tiles_q, naux, LANES), jnp.float32),
            jax.ShapeDtypeStruct((2, naux, LANES), jnp.float32),
        ],
        in_specs=[anywhere] * 3,
        out_specs=[vmem] * 2,
        scratch_shapes=[
            pltpu.VMEM((naux * occ_local, nvirt), jnp.bfloat16),
            pltpu.VMEM((occ_local, width), jnp.bfloat16),
            pltpu.VMEM((nchunks, nvirt, CHUNK), jnp.bfloat16),
            pltpu.VMEM((tiles_q, naux, LANES), jnp.float32),
            pltpu.VMEM((nchunks, PLANE, TILE_P, LANES), jnp.float32),
            pltpu.VMEM((nchunks, TILE_P, LANES), jnp.float32),
            pltpu.SemaphoreType.DMA((2 + nchunks,)),
            pltpu.SemaphoreType.DMA((nchunks, 12)),
            pltpu.SemaphoreType.DMA((nchunks,)),
            pltpu.SemaphoreType.DMA,
            pltpu.SemaphoreType.DMA((nchunks,)),
            pltpu.SemaphoreType.DMA,
            pltpu.SemaphoreType.DMA((nchunks,)),
            pltpu.SemaphoreType.DMA,
            pltpu.SemaphoreType.REGULAR((3,)),
        ],
        compiler_params=pltpu.CompilerParams(
            collective_id=0, has_side_effects=True, vmem_limit_bytes=56 * 2**20
        ),
        cost_estimate=pl.CostEstimate(
            flops=2 * naux * occ_local * nvirt * width, bytes_accessed=12 * 2**20, transcendentals=0
        ),
        name="project",
    )(flat, occupied_points, virtual_points)
    transposed = pl.pallas_call(
        gram_kernel,
        out_shape=jax.ShapeDtypeStruct((tile_width, width), jnp.float32),
        in_specs=[vmem] * 2,
        out_specs=vmem,
        cost_estimate=pl.CostEstimate(
            flops=12 * naux * width * tile_width, bytes_accessed=2**20, transcendentals=0
        ),
        name="gram",
    )(rows, cols)
    return transposed.T


def solution(mesh):
    return jax.shard_map(
        body,
        mesh=mesh,
        in_specs=(P(None, "occ", None), P("occ", "pts"), P("occ", "pts")),
        out_specs=P("pts", "occ"),
        check_vma=False,
    )
```

```python
import functools

import jax
import jax.numpy as jnp
from jax import lax
from jax.experimental import pallas as pl
from jax.experimental.pallas import tpu as pltpu
from jax.sharding import PartitionSpec as P

MESH = pl.DeviceIdType.MESH
NX, NY, NZ = 4, 4, 8
PLANE = NX * NY * 2
CHUNK = 256
LANES = 128
TILE_P = 8


def split3(x):
    hi = x.astype(jnp.bfloat16)
    rest = x - hi.astype(jnp.float32)
    mid = rest.astype(jnp.bfloat16)
    low = (rest - mid.astype(jnp.float32)).astype(jnp.bfloat16)
    return hi, mid, low


def kernel(b_hbm, occ_hbm, v_hbm, rows_y, cols_y, b_ref, occ_ref, panel, part, gathered, total,
           local_sem, recv_sem, send_sem, rs_send, rs_recv, ag_send, ag_recv, col_recv, z_token):
    nrows, width = v_hbm.shape
    nchunks = width // CHUNK
    blocks = CHUNK // LANES
    naux = part.shape[1]
    groups = naux // TILE_P
    tiles = blocks * groups
    last = nchunks - 1
    occ_local = occ_ref.shape[0]

    me = lax.axis_index("occ")
    z = lax.axis_index("pts")
    core = lax.rem(me, 2)
    x = lax.rem(me // 2, NX)
    y = me // (2 * NX)
    first = x + core * (y - x)
    second = y + core * (x - y)

    def occ_of(f, s):
        f = lax.rem(first + f + 4, 4)
        s = lax.rem(second + s + 4, 4)
        return (s * (4 - 3 * core) + f * (1 + 3 * core)) * 2 + core

    def at(f, s):
        return {"occ": occ_of(f, s), "pts": z}

    sibling = {"occ": me + 1 - 2 * core, "pts": z}
    above = {"occ": me, "pts": lax.rem(z + 1, NZ)}
    below = {"occ": me, "pts": lax.rem(z + NZ - 1, NZ)}

    home = me // 4
    tile = lax.rem(me, 4)
    first_block = 3 * (tile // 2) + lax.rem(tile, 2)
    is_home = home == z

    my_chunk = lax.rem(me, 4)
    my_tile = me // 4
    home_x = 2 * lax.rem(z, 2) + 1
    home_y = z // 2
    home_dy = lax.rem(y + NY - home_y, NY)
    last_tile = 2 * lax.rem(x + NX - home_x + 2 * home_dy, NX) + core
    sends_columns = jnp.logical_or(
        jnp.logical_and(home_dy == 0, last_tile // 2 != 2), jnp.logical_and(home_dy == 1, last_tile // 2 == 2)
    )

    barrier = pltpu.get_barrier_semaphore()
    neighbours = [at(1, 0), at(-1, 0), at(0, 1), at(0, -1), sibling, above, below]
    for device in neighbours:
        pl.semaphore_signal(barrier, inc=1, device_id=device, device_id_type=MESH)

    b_copy = pltpu.make_async_copy(b_hbm, b_ref, local_sem.at[0])
    occ_copy = pltpu.make_async_copy(occ_hbm, occ_ref, local_sem.at[1])
    own_copies = [
        pltpu.make_async_copy(
            v_hbm.at[:, pl.ds(k * CHUNK, CHUNK)], panel.at[k, pl.ds(me * nrows, nrows)], local_sem.at[2 + k]
        )
        for k in range(nchunks)
    ]
    for copy in own_copies:
        copy.start()

    pl.semaphore_wait(barrier, len(neighbours))

    def z_signal(r):
        for device in (above, below):
            pl.semaphore_signal(z_token.at[r], inc=1, device_id=device, device_id_type=MESH)

    def z_wait(r):
        pl.semaphore_wait(z_token.at[r], 2)

    half = nrows // 32 * 16 + 16 if nrows % 32 else nrows // 2

    def push(k, row, count, device, slot):
        block = panel.at[k, pl.ds(row, count)]
        pltpu.make_async_remote_copy(
            src_ref=block,
            dst_ref=block,
            send_sem=send_sem.at[k],
            recv_sem=recv_sem.at[k, slot],
            device_id=device,
            device_id_type=MESH,
        ).start()

    def row_of(f, s):
        return pl.multiple_of(occ_of(f, s) * nrows, 16)

    def shard(k, f, s, device, slot):
        push(k, row_of(f, s), nrows, device, slot)

    def arrived(k, slot, count):
        block = panel.at[k, pl.ds(0, count)]
        pltpu.make_async_copy(block, block, recv_sem.at[k, slot]).wait()

    def phase0(k):
        own_copies[k].wait()
        shard(k, 0, 0, at(1, 0), 0)
        shard(k, 0, 0, at(-1, 0), 1)
        shard(k, 0, 0, sibling, 10)

    def halves(k):
        arrived(k, 0, nrows)
        push(k, row_of(-1, 0), half, at(1, 0), 2)
        arrived(k, 1, nrows)
        push(k, pl.multiple_of(row_of(1, 0) + half, 16), nrows - half, at(-1, 0), 3)

    def bulk(k):
        shard(k, 1, 0, at(0, -1), 6)
        for f in (0, -1):
            shard(k, f, 0, at(0, 1), 4)
        for f in (0, -1):
            shard(k, f, 0, at(0, -1), 7)
        shard(k, 1, 0, at(0, 1), 5)
        shard(k, 1, 0, sibling, 10)
        shard(k, -1, 0, sibling, 10)

    def opposite(k):
        arrived(k, 2, half)
        arrived(k, 3, nrows - half)
        shard(k, 2, 0, at(0, -1), 11)
        shard(k, 2, 0, at(0, 1), 5)
        shard(k, 2, 0, sibling, 10)

    def phase3a(k):
        arrived(k, 4, 2 * nrows)
        for f in (0, -1):
            shard(k, f, -1, at(0, 1), 8)
        arrived(k, 6, nrows)
        shard(k, 1, 1, at(0, -1), 9)
        for f in (0, -1):
            shard(k, f, -1, sibling, 10)
        shard(k, 1, 1, sibling, 10)

    def phase3b(k):
        arrived(k, 11, nrows)
        shard(k, 2, 1, at(0, -1), 9)
        shard(k, 2, 1, sibling, 10)

    def phase3c(k):
        arrived(k, 5, 2 * nrows)
        for f in (1, 2):
            shard(k, f, -1, sibling, 10)
        arrived(k, 7, 2 * nrows)
        for f in (0, -1):
            shard(k, f, 1, sibling, 10)

    def phase3(k):
        phase3a(k)
        phase3b(k)
        phase3c(k)

    def phase4a(k):
        arrived(k, 8, 2 * nrows)
        for f in (0, -1):
            shard(k, f, 2, sibling, 10)

    def phase4b(k):
        arrived(k, 9, 2 * nrows)
        for f in (1, 2):
            shard(k, f, 2, sibling, 10)

    def phase4(k):
        phase4a(k)
        phase4b(k)

    def phase5(k):
        arrived(k, 10, PLANE // 2 * nrows)

    def compute(k, g):
        depth = TILE_P * occ_local
        t = jnp.dot(b_ref[pl.ds(g * depth, depth), :], panel[k], preferred_element_type=jnp.float32)
        o = occ_ref[:, pl.ds(k * CHUNK, CHUNK)].astype(jnp.float32)
        sums = jnp.sum(t.reshape(TILE_P, occ_local, CHUNK) * o[None], axis=1)
        for h in range(blocks):
            part[k * blocks + h, pl.ds(g * TILE_P, TILE_P)] = sums[:, h * LANES:(h + 1) * LANES]

    def multiply(k):
        for g in range(groups):
            compute(k, g)

    def tile_of(ref, k, t):
        if isinstance(t, int):
            return ref.at[k * blocks + t // groups, pl.ds(t % groups * TILE_P, TILE_P)]
        return ref.at[k * blocks + t // groups, pl.ds(pl.multiple_of(lax.rem(t, groups) * TILE_P, TILE_P), TILE_P)]

    def send(src, dst, ssem, rsem, occ, pts):
        pltpu.make_async_remote_copy(
            src_ref=src, dst_ref=dst, send_sem=ssem, recv_sem=rsem,
            device_id={"occ": occ, "pts": pts}, device_id_type=MESH,
        ).start()

    def send_part(k, t, owner):
        send(tile_of(part, k, t), gathered.at[k, lax.rem(me - owner + PLANE, PLANE) - 1],
             rs_send, rs_recv.at[k], owner, z)

    def scatter(k):
        def step(n, _):
            t = lax.rem(my_tile + n, tiles)
            send_part(k, t, t * 4 + k)
            return 0

        lax.fori_loop(jnp.where(my_chunk == k, 1, 0), tiles, step, 0)

    def scatter_last(first_group, last_group):
        for t in range(tiles):
            if not first_group <= t % groups < last_group:
                continue
            for r in (2, 1, 3, 0):
                column = lax.rem(home_x + t // 2 + 2 * (home_dy + r), NX)
                owner = (lax.rem(y + r, NY) * NX + column) * 2 + t % 2
                if r:
                    send_part(last, t, owner)
                else:
                    @pl.when(last_tile != t)
                    def _():
                        send_part(last, t, owner)

    def wait_tiles(sem, count):
        block = gathered.at[0, pl.ds(0, count)]
        pltpu.make_async_copy(block, block, sem).wait()

    def add_up(k, t):
        wait_tiles(rs_recv.at[k], PLANE - 1)
        acc = tile_of(part, k, t)[...]
        for n in range(PLANE - 1):
            acc = acc + gathered[k, n]
        total[k] = acc
        tile_of(rows_y, k, t)[...] = acc

    def to_columns(k, t):
        block = k * blocks + t // groups
        low = 2 * (block // 3) + lax.rem(block, 3) // 2

        def to_user(user):
            slot = block - (3 * (user // 2) + lax.rem(user, 2))
            for n in (4, 3, 5, 2, 6, 1, 7):
                send(total.at[k],
                     cols_y.at[slot, pl.ds(pl.multiple_of(lax.rem(t, groups) * TILE_P, TILE_P), TILE_P)],
                     ag_send, col_recv, z * 4 + user, lax.rem(z + n, NZ))

        to_user(low)

        @pl.when(lax.rem(block, 3) == 1)
        def _():
            to_user(low + 1)

    def spread(k):
        add_up(k, my_tile)
        to_columns(k, my_tile)

        def step(n, _):
            send(total.at[k], tile_of(rows_y, k, my_tile), ag_send, ag_recv.at[k], lax.rem(me + n, PLANE), z)
            return 0

        lax.fori_loop(1, PLANE, step, 0)

    def spread_last():
        add_up(last, last_tile)

        @pl.when(sends_columns)
        def _():
            to_columns(last, last_tile)

        def step(n, _):
            send(total.at[last], tile_of(rows_y, last, last_tile), ag_send, ag_recv.at[last],
                 y * 2 * NX + lax.rem(x * 2 + core + n, 2 * NX), z)
            return 0

        lax.fori_loop(1, 2 * NX, step, 0)

    def columns_sent(k, t):
        wait_tiles(ag_send, NZ - 1)

        @pl.when(lax.rem(k * blocks + t // groups, 3) == 1)
        def _():
            wait_tiles(ag_send, NZ - 1)

    z_signal(0)
    phase0(0)
    phase0(1)
    phase0(2)
    b_copy.start()
    occ_copy.start()
    halves(0)
    bulk(0)
    halves(1)
    bulk(1)
    halves(2)
    opposite(0)
    opposite(1)
    z_wait(0)
    z_signal(1)
    phase3(0)
    opposite(2)
    bulk(2)
    phase3(1)
    z_wait(1)
    z_signal(2)
    b_copy.wait()
    occ_copy.wait()
    phase4(0)
    phase5(0)
    multiply(0)
    phase3a(2)
    phase3b(2)
    phase3c(2)
    phase4(1)
    z_wait(2)
    scatter(0)
    phase5(1)
    compute(1, 0)
    compute(1, 1)
    phase4a(2)
    phase4b(2)
    compute(1, 2)
    compute(1, 3)
    phase5(2)
    scatter(1)
    multiply(2)
    scatter_last(0, groups)

    for k in range(last):
        @pl.when(my_chunk == k)
        def _():
            spread(k)

    spread_last()

    for k in range(last):
        @pl.when(my_chunk == k)
        def _():
            wait_tiles(ag_recv.at[k], tiles - 1)

        @pl.when(my_chunk != k)
        def _():
            wait_tiles(ag_recv.at[k], tiles)

    wait_tiles(ag_recv.at[last], tiles - 1)

    @pl.when(is_home)
    def _():
        cols_y[...] = rows_y[pl.ds(first_block, 2)]

    @pl.when(jnp.logical_not(is_home))
    def _():
        wait_tiles(col_recv, 2 * groups)

    for k in range(nchunks):
        sent = panel.at[k, pl.ds(0, (PLANE - 1) * nrows)]
        pltpu.make_async_copy(sent, sent, send_sem.at[k]).wait()

    wait_tiles(rs_send, PLANE - 1)
    for k in range(last):
        @pl.when(my_chunk == k)
        def _():
            wait_tiles(rs_send, tiles - 1)
            wait_tiles(ag_send, PLANE - 1)
            columns_sent(k, my_tile)

        @pl.when(my_chunk != k)
        def _():
            wait_tiles(rs_send, tiles)

    wait_tiles(ag_send, tiles - 1)

    @pl.when(sends_columns)
    def _():
        columns_sent(last, last_tile)


def gram_kernel(rows_ref, cols_ref, out_ref):
    odd = lax.rem(lax.axis_index("occ"), 2) == 1
    cols = jnp.concatenate([cols_ref[0], cols_ref[1]], axis=1)
    cols = jnp.where(odd, pltpu.roll(cols, cols.shape[1] - LANES // 2, 1), cols)
    c1, c2, c3 = split3(cols)
    right = jnp.concatenate([c1, c2, c1, c2, c3, c1], axis=0)
    for qb in range(rows_ref.shape[0]):
        r1, r2, r3 = split3(rows_ref[qb])
        left = jnp.concatenate([r1, r1, r2, r2, r1, r3], axis=0)
        g = lax.dot_general(right, left, (((0,), (0,)), ((), ())), preferred_element_type=jnp.float32)
        out_ref[:, pl.ds(qb * LANES, LANES)] = g[:out_ref.shape[0]]


def body(integrals, occupied_points, virtual_points):
    naux, occ_local, nvirt = integrals.shape
    nrows, width = virtual_points.shape
    nchunks = width // CHUNK
    tiles_q = width // LANES
    tile_width = width * NZ // PLANE
    flat = integrals.reshape(naux * occ_local, nvirt)
    anywhere = pl.BlockSpec(memory_space=pl.ANY)
    vmem = pl.BlockSpec(memory_space=pltpu.VMEM)
    rows, cols = pl.pallas_call(
        kernel,
        out_shape=[
            jax.ShapeDtypeStruct((tiles_q, naux, LANES), jnp.float32),
            jax.ShapeDtypeStruct((2, naux, LANES), jnp.float32),
        ],
        in_specs=[anywhere] * 3,
        out_specs=[vmem] * 2,
        scratch_shapes=[
            pltpu.VMEM((naux * occ_local, nvirt), jnp.bfloat16),
            pltpu.VMEM((occ_local, width), jnp.bfloat16),
            pltpu.VMEM((nchunks, nvirt, CHUNK), jnp.bfloat16),
            pltpu.VMEM((tiles_q, naux, LANES), jnp.float32),
            pltpu.VMEM((nchunks, PLANE, TILE_P, LANES), jnp.float32),
            pltpu.VMEM((nchunks, TILE_P, LANES), jnp.float32),
            pltpu.SemaphoreType.DMA((2 + nchunks,)),
            pltpu.SemaphoreType.DMA((nchunks, 12)),
            pltpu.SemaphoreType.DMA((nchunks,)),
            pltpu.SemaphoreType.DMA,
            pltpu.SemaphoreType.DMA((nchunks,)),
            pltpu.SemaphoreType.DMA,
            pltpu.SemaphoreType.DMA((nchunks,)),
            pltpu.SemaphoreType.DMA,
            pltpu.SemaphoreType.REGULAR((3,)),
        ],
        compiler_params=pltpu.CompilerParams(
            collective_id=0, has_side_effects=True, vmem_limit_bytes=56 * 2**20
        ),
        cost_estimate=pl.CostEstimate(
            flops=2 * naux * occ_local * nvirt * width, bytes_accessed=12 * 2**20, transcendentals=0
        ),
        name="project",
    )(flat, occupied_points, virtual_points)
    transposed = pl.pallas_call(
        gram_kernel,
        out_shape=jax.ShapeDtypeStruct((tile_width, width), jnp.float32),
        in_specs=[vmem] * 2,
        out_specs=vmem,
        cost_estimate=pl.CostEstimate(
            flops=12 * naux * width * tile_width, bytes_accessed=2**20, transcendentals=0
        ),
        name="gram",
    )(rows, cols)
    return transposed.T


def solution(mesh):
    return jax.shard_map(
        body,
        mesh=mesh,
        in_specs=(P(None, "occ", None), P("occ", "pts"), P("occ", "pts")),
        out_specs=P("pts", "occ"),
        check_vma=False,
    )
```

```python
import functools

import jax
import jax.numpy as jnp
from jax import lax
from jax.experimental import pallas as pl
from jax.experimental.pallas import tpu as pltpu
from jax.sharding import PartitionSpec as P

MESH = pl.DeviceIdType.MESH
NX, NY, NZ = 4, 4, 8
PLANE = NX * NY * 2
CHUNK = 256
LANES = 128
TILE_P = 8
REPLICAS = 2


def split3(x):
    hi = x.astype(jnp.bfloat16)
    rest = x - hi.astype(jnp.float32)
    mid = rest.astype(jnp.bfloat16)
    low = (rest - mid.astype(jnp.float32)).astype(jnp.bfloat16)
    return hi, mid, low


def kernel(b_hbm, occ_hbm, v_hbm, rows_y, cols_y, b_ref, occ_ref, panel, part, gathered, total,
           local_sem, recv_sem, send_sem, rs_send, rs_recv, ag_send, ag_recv, col_recv, z_token):
    nrows, width = v_hbm.shape
    nchunks = width // CHUNK
    blocks = CHUNK // LANES
    naux = part.shape[1]
    groups = naux // TILE_P
    tiles = blocks * groups
    last = nchunks - 1
    occ_local = occ_ref.shape[0]

    me = lax.axis_index("occ")
    z = lax.axis_index("pts")
    core = lax.rem(me, 2)
    x = lax.rem(me // 2, NX)
    y = me // (2 * NX)
    first = x + core * (y - x)
    second = y + core * (x - y)

    def occ_of(f, s):
        f = lax.rem(first + f + 4, 4)
        s = lax.rem(second + s + 4, 4)
        return (s * (4 - 3 * core) + f * (1 + 3 * core)) * 2 + core

    def at(f, s):
        return {"occ": occ_of(f, s), "pts": z}

    sibling = {"occ": me + 1 - 2 * core, "pts": z}
    above = {"occ": me, "pts": lax.rem(z + 1, NZ)}
    below = {"occ": me, "pts": lax.rem(z + NZ - 1, NZ)}

    home = me // 4
    tile = lax.rem(me, 4)
    first_block = 3 * (tile // 2) + lax.rem(tile, 2)
    is_home = home == z

    my_chunk = lax.rem(me, 4)
    my_tile = me // 4
    home_x = 2 * lax.rem(z, 2) + 1
    home_y = z // 2
    home_dy = lax.rem(y + NY - home_y, NY)
    last_tile = 2 * lax.rem(x + NX - home_x + 2 * home_dy, NX) + core
    owns_last = home_dy < REPLICAS
    sends_columns = jnp.logical_or(
        jnp.logical_and(home_dy == 0, last_tile // 2 != 2), jnp.logical_and(home_dy == 1, last_tile // 2 == 2)
    )

    barrier = pltpu.get_barrier_semaphore()
    neighbours = [at(1, 0), at(-1, 0), at(0, 1), at(0, -1), sibling, above, below]
    for device in neighbours:
        pl.semaphore_signal(barrier, inc=1, device_id=device, device_id_type=MESH)

    b_copy = pltpu.make_async_copy(b_hbm, b_ref, local_sem.at[0])
    occ_copy = pltpu.make_async_copy(occ_hbm, occ_ref, local_sem.at[1])
    own_copies = [
        pltpu.make_async_copy(
            v_hbm.at[:, pl.ds(k * CHUNK, CHUNK)], panel.at[k, pl.ds(me * nrows, nrows)], local_sem.at[2 + k]
        )
        for k in range(nchunks)
    ]
    for copy in own_copies:
        copy.start()

    pl.semaphore_wait(barrier, len(neighbours))

    def z_signal(r):
        for device in (above, below):
            pl.semaphore_signal(z_token.at[r], inc=1, device_id=device, device_id_type=MESH)

    def z_wait(r):
        pl.semaphore_wait(z_token.at[r], 2)

    half = nrows // 32 * 16 + 16 if nrows % 32 else nrows // 2

    def push(k, row, count, device, slot):
        block = panel.at[k, pl.ds(row, count)]
        pltpu.make_async_remote_copy(
            src_ref=block,
            dst_ref=block,
            send_sem=send_sem.at[k],
            recv_sem=recv_sem.at[k, slot],
            device_id=device,
            device_id_type=MESH,
        ).start()

    def row_of(f, s):
        return pl.multiple_of(occ_of(f, s) * nrows, 16)

    def shard(k, f, s, device, slot):
        push(k, row_of(f, s), nrows, device, slot)

    def arrived(k, slot, count):
        block = panel.at[k, pl.ds(0, count)]
        pltpu.make_async_copy(block, block, recv_sem.at[k, slot]).wait()

    def phase0(k):
        own_copies[k].wait()
        shard(k, 0, 0, at(1, 0), 0)
        shard(k, 0, 0, at(-1, 0), 1)
        shard(k, 0, 0, sibling, 10)

    def halves(k):
        arrived(k, 0, nrows)
        push(k, row_of(-1, 0), half, at(1, 0), 2)
        arrived(k, 1, nrows)
        push(k, pl.multiple_of(row_of(1, 0) + half, 16), nrows - half, at(-1, 0), 3)

    def bulk(k):
        shard(k, 1, 0, at(0, -1), 6)
        for f in (0, -1):
            shard(k, f, 0, at(0, 1), 4)
        for f in (0, -1):
            shard(k, f, 0, at(0, -1), 7)
        shard(k, 1, 0, at(0, 1), 5)
        shard(k, 1, 0, sibling, 10)
        shard(k, -1, 0, sibling, 10)

    def opposite(k):
        arrived(k, 2, half)
        arrived(k, 3, nrows - half)
        shard(k, 2, 0, at(0, -1), 11)
        shard(k, 2, 0, at(0, 1), 5)
        shard(k, 2, 0, sibling, 10)

    def phase3a(k):
        arrived(k, 4, 2 * nrows)
        for f in (0, -1):
            shard(k, f, -1, at(0, 1), 8)
        arrived(k, 6, nrows)
        shard(k, 1, 1, at(0, -1), 9)
        for f in (0, -1):
            shard(k, f, -1, sibling, 10)
        shard(k, 1, 1, sibling, 10)

    def phase3b(k):
        arrived(k, 11, nrows)
        shard(k, 2, 1, at(0, -1), 9)
        shard(k, 2, 1, sibling, 10)

    def phase3c(k):
        arrived(k, 5, 2 * nrows)
        for f in (1, 2):
            shard(k, f, -1, sibling, 10)
        arrived(k, 7, 2 * nrows)
        for f in (0, -1):
            shard(k, f, 1, sibling, 10)

    def phase3(k):
        phase3a(k)
        phase3b(k)
        phase3c(k)

    def phase4a(k):
        arrived(k, 8, 2 * nrows)
        for f in (0, -1):
            shard(k, f, 2, sibling, 10)

    def phase4b(k):
        arrived(k, 9, 2 * nrows)
        for f in (1, 2):
            shard(k, f, 2, sibling, 10)

    def phase4(k):
        phase4a(k)
        phase4b(k)

    def phase5(k):
        arrived(k, 10, PLANE // 2 * nrows)

    def compute(k, g):
        depth = TILE_P * occ_local
        t = jnp.dot(b_ref[pl.ds(g * depth, depth), :], panel[k], preferred_element_type=jnp.float32)
        o = occ_ref[:, pl.ds(k * CHUNK, CHUNK)].astype(jnp.float32)
        sums = jnp.sum(t.reshape(TILE_P, occ_local, CHUNK) * o[None], axis=1)
        for h in range(blocks):
            part[k * blocks + h, pl.ds(g * TILE_P, TILE_P)] = sums[:, h * LANES:(h + 1) * LANES]

    def multiply(k):
        for g in range(groups):
            compute(k, g)

    def tile_of(ref, k, t):
        if isinstance(t, int):
            return ref.at[k * blocks + t // groups, pl.ds(t % groups * TILE_P, TILE_P)]
        return ref.at[k * blocks + t // groups, pl.ds(pl.multiple_of(lax.rem(t, groups) * TILE_P, TILE_P), TILE_P)]

    def send(src, dst, ssem, rsem, occ, pts):
        pltpu.make_async_remote_copy(
            src_ref=src, dst_ref=dst, send_sem=ssem, recv_sem=rsem,
            device_id={"occ": occ, "pts": pts}, device_id_type=MESH,
        ).start()

    def send_part(k, t, owner):
        send(tile_of(part, k, t), gathered.at[k, lax.rem(me - owner + PLANE, PLANE) - 1],
             rs_send, rs_recv.at[k], owner, z)

    def scatter(k):
        def step(n, _):
            t = lax.rem(my_tile + n, tiles)
            send_part(k, t, t * 4 + k)
            return 0

        lax.fori_loop(jnp.where(my_chunk == k, 1, 0), tiles, step, 0)

    def scatter_last():
        for d in range(REPLICAS):
            for t in range(tiles):
                column = lax.rem(home_x + t // 2 + 2 * d, NX)
                owner = (lax.rem(home_y + d, NY) * NX + column) * 2 + t % 2

                @pl.when(owner != me)
                def _():
                    send_part(last, t, owner)

    def wait_tiles(sem, count):
        block = gathered.at[0, pl.ds(0, count)]
        pltpu.make_async_copy(block, block, sem).wait()

    def add_up(k, t):
        wait_tiles(rs_recv.at[k], PLANE - 1)
        acc = tile_of(part, k, t)[...]
        for n in range(PLANE - 1):
            acc = acc + gathered[k, n]
        total[k] = acc
        tile_of(rows_y, k, t)[...] = acc

    def to_columns(k, t):
        block = k * blocks + t // groups
        low = 2 * (block // 3) + lax.rem(block, 3) // 2

        def to_user(user):
            slot = block - (3 * (user // 2) + lax.rem(user, 2))
            for n in (4, 3, 5, 2, 6, 1, 7):
                send(total.at[k],
                     cols_y.at[slot, pl.ds(pl.multiple_of(lax.rem(t, groups) * TILE_P, TILE_P), TILE_P)],
                     ag_send, col_recv, z * 4 + user, lax.rem(z + n, NZ))

        to_user(low)

        @pl.when(lax.rem(block, 3) == 1)
        def _():
            to_user(low + 1)

    def spread(k):
        add_up(k, my_tile)
        to_columns(k, my_tile)

        def step(n, _):
            send(total.at[k], tile_of(rows_y, k, my_tile), ag_send, ag_recv.at[k], lax.rem(me + n, PLANE), z)
            return 0

        lax.fori_loop(1, PLANE, step, 0)

    def spread_last():
        add_up(last, last_tile)

        @pl.when(sends_columns)
        def _():
            to_columns(last, last_tile)

        for row in range(NY // REPLICAS - 1, -1, -1):
            def step(n, _):
                send(total.at[last], tile_of(rows_y, last, last_tile), ag_send, ag_recv.at[last],
                     lax.rem(y + row * REPLICAS, NY) * 2 * NX + lax.rem(x * 2 + core + n, 2 * NX), z)
                return 0

            lax.fori_loop(0 if row else 1, 2 * NX, step, 0)

    def columns_sent(k, t):
        wait_tiles(ag_send, NZ - 1)

        @pl.when(lax.rem(k * blocks + t // groups, 3) == 1)
        def _():
            wait_tiles(ag_send, NZ - 1)

    z_signal(0)
    phase0(0)
    phase0(1)
    phase0(2)
    b_copy.start()
    occ_copy.start()
    halves(0)
    bulk(0)
    halves(1)
    bulk(1)
    halves(2)
    opposite(0)
    opposite(1)
    z_wait(0)
    z_signal(1)
    phase3(0)
    opposite(2)
    bulk(2)
    phase3(1)
    z_wait(1)
    z_signal(2)
    b_copy.wait()
    occ_copy.wait()
    phase4(0)
    phase5(0)
    multiply(0)
    phase3a(2)
    phase3b(2)
    phase3c(2)
    phase4(1)
    phase5(1)
    compute(1, 0)
    compute(1, 1)
    phase4a(2)
    phase4b(2)
    compute(1, 2)
    compute(1, 3)
    z_wait(2)
    scatter(0)
    scatter(1)
    phase5(2)
    multiply(2)
    scatter_last()

    for k in range(last):
        @pl.when(my_chunk == k)
        def _():
            spread(k)

    @pl.when(owns_last)
    def _():
        spread_last()

    for k in range(last):
        @pl.when(my_chunk == k)
        def _():
            wait_tiles(ag_recv.at[k], tiles - 1)

        @pl.when(my_chunk != k)
        def _():
            wait_tiles(ag_recv.at[k], tiles)

    @pl.when(owns_last)
    def _():
        wait_tiles(ag_recv.at[last], tiles - 1)

    @pl.when(jnp.logical_not(owns_last))
    def _():
        wait_tiles(ag_recv.at[last], tiles)

    @pl.when(is_home)
    def _():
        cols_y[...] = rows_y[pl.ds(first_block, 2)]

    @pl.when(jnp.logical_not(is_home))
    def _():
        wait_tiles(col_recv, 2 * groups)

    for k in range(nchunks):
        sent = panel.at[k, pl.ds(0, (PLANE - 1) * nrows)]
        pltpu.make_async_copy(sent, sent, send_sem.at[k]).wait()

    @pl.when(owns_last)
    def _():
        wait_tiles(rs_send, REPLICAS * tiles - 1)
        wait_tiles(ag_send, NY // REPLICAS * tiles - 1)

    @pl.when(jnp.logical_not(owns_last))
    def _():
        wait_tiles(rs_send, REPLICAS * tiles)

    for k in range(last):
        @pl.when(my_chunk == k)
        def _():
            wait_tiles(rs_send, tiles - 1)
            wait_tiles(ag_send, PLANE - 1)
            columns_sent(k, my_tile)

        @pl.when(my_chunk != k)
        def _():
            wait_tiles(rs_send, tiles)

    @pl.when(sends_columns)
    def _():
        columns_sent(last, last_tile)


def gram_kernel(rows_ref, cols_ref, out_ref):
    odd = lax.rem(lax.axis_index("occ"), 2) == 1
    cols = jnp.concatenate([cols_ref[0], cols_ref[1]], axis=1)
    cols = jnp.where(odd, pltpu.roll(cols, cols.shape[1] - LANES // 2, 1), cols)
    c1, c2, c3 = split3(cols)
    right = jnp.concatenate([c1, c2, c1, c2, c3, c1], axis=0).T[:out_ref.shape[0]]
    for qb in range(0, rows_ref.shape[0], 2):
        r1, r2, r3 = split3(jnp.concatenate([rows_ref[qb], rows_ref[qb + 1]], axis=1))
        left = jnp.concatenate([r1, r1, r2, r2, r1, r3], axis=0)
        g = jnp.dot(right, left, preferred_element_type=jnp.float32)
        out_ref[:, pl.ds(qb * LANES, 2 * LANES)] = g


def body(integrals, occupied_points, virtual_points):
    naux, occ_local, nvirt = integrals.shape
    nrows, width = virtual_points.shape
    nchunks = width // CHUNK
    tiles_q = width // LANES
    tile_width = width * NZ // PLANE
    flat = integrals.reshape(naux * occ_local, nvirt)
    anywhere = pl.BlockSpec(memory_space=pl.ANY)
    vmem = pl.BlockSpec(memory_space=pltpu.VMEM)
    rows, cols = pl.pallas_call(
        kernel,
        out_shape=[
            jax.ShapeDtypeStruct((tiles_q, naux, LANES), jnp.float32),
            jax.ShapeDtypeStruct((2, naux, LANES), jnp.float32),
        ],
        in_specs=[anywhere] * 3,
        out_specs=[vmem] * 2,
        scratch_shapes=[
            pltpu.VMEM((naux * occ_local, nvirt), jnp.bfloat16),
            pltpu.VMEM((occ_local, width), jnp.bfloat16),
            pltpu.VMEM((nchunks, nvirt, CHUNK), jnp.bfloat16),
            pltpu.VMEM((tiles_q, naux, LANES), jnp.float32),
            pltpu.VMEM((nchunks, PLANE, TILE_P, LANES), jnp.float32),
            pltpu.VMEM((nchunks, TILE_P, LANES), jnp.float32),
            pltpu.SemaphoreType.DMA((2 + nchunks,)),
            pltpu.SemaphoreType.DMA((nchunks, 12)),
            pltpu.SemaphoreType.DMA((nchunks,)),
            pltpu.SemaphoreType.DMA,
            pltpu.SemaphoreType.DMA((nchunks,)),
            pltpu.SemaphoreType.DMA,
            pltpu.SemaphoreType.DMA((nchunks,)),
            pltpu.SemaphoreType.DMA,
            pltpu.SemaphoreType.REGULAR((3,)),
        ],
        compiler_params=pltpu.CompilerParams(
            collective_id=0, has_side_effects=True, vmem_limit_bytes=56 * 2**20
        ),
        cost_estimate=pl.CostEstimate(
            flops=2 * naux * occ_local * nvirt * width, bytes_accessed=12 * 2**20, transcendentals=0
        ),
        name="project",
    )(flat, occupied_points, virtual_points)
    transposed = pl.pallas_call(
        gram_kernel,
        out_shape=jax.ShapeDtypeStruct((tile_width, width), jnp.float32),
        in_specs=[vmem] * 2,
        out_specs=vmem,
        cost_estimate=pl.CostEstimate(
            flops=12 * naux * width * tile_width, bytes_accessed=2**20, transcendentals=0
        ),
        name="gram",
    )(rows, cols)
    return transposed.T


def solution(mesh):
    return jax.shard_map(
        body,
        mesh=mesh,
        in_specs=(P(None, "occ", None), P("occ", "pts"), P("occ", "pts")),
        out_specs=P("pts", "occ"),
        check_vma=False,
    )
```
